32 devices in a mesh: rows: 8 (over z, y), cols: 4 (over x, core).
Axes of the slice: x: 2, y: 2, z: 4, core: 2. Of those that a mesh axis runs over, the one named last changes fastest.
Arguments:
- coupling: float32 [4096, 8192], P('rows', 'cols'), may hold values from 0.1 to 10, as said below
- source: float32 [4096, 256], P('rows'), may hold values from -150 to 150
- target: float32 [8192, 256], P('cols'), may hold values from -6 to 6
Outputs:
- log_coupling: float32 [4096, 8192], P('rows', 'cols')
The draws below stay inside these ranges and needn't reach their ends.
Inputs may be any that keep to these rules, and one draw needn't show every extreme that they name: `coupling`: positive entries.
All inputs are finite; a program needn't handle non-finite values.
Results may differ from the reference program's by a relative error of at most 0.0003.
Values sent between devices are 32-bit elements; how exact they have to be, the bound alone decides.
A program may use at most 64 MiB of HBM per device.

```python
import math
import jax
import jax.numpy as jnp
from jax import lax

R = 256
SWEEPS = 3
N = 4096
M = 8192


def draw_source(key, part):
    key = jax.random.fold_in(key, 11)
    keys = jax.random.split(key, 1)
    base = jnp.clip(jax.random.normal(keys[0], (N, R), jnp.float32), -6.0, 6.0)
    return base


def draw_coupling(key, part):
    key = jax.random.fold_in(key, 23)
    keys = jax.random.split(key, 1)
    return jnp.exp(jax.random.uniform(keys[0], (N, M), jnp.float32, -2.3, 2.3))


def block_levels(key, dims, cuts, low, top_value):
    loudness, own = 1.0, jax.random.fold_in(key, 6)
    for axis_at, shards_of in cuts:
        heights = jnp.exp(jax.random.uniform(jax.random.fold_in(own, axis_at), (shards_of,), jnp.float32, low / len(cuts), top_value / len(cuts)))
        loudness = loudness * jnp.repeat(heights, dims[axis_at] // shards_of).reshape([-1 if axis == axis_at else 1 for axis in range(len(dims))])
    return loudness


def noise(key, dims, width, most, pieces=(), held_as=jnp.bfloat16):
    array = jax.random.normal(key, dims, jnp.float32) * width
    if len(pieces) > 0:
        array = block_levels(key, dims, pieces, -0.22, 0.18) * array
    return jnp.clip(array, min=-most, max=most).astype(held_as)


def setup_inputs(seed: int = 0) -> dict:
    splits = jax.random.split(jax.random.key(seed), 4)
    return {
        "coupling": draw_coupling(jax.random.fold_in(splits[3], 71), 0),
        "source": draw_source(jax.random.fold_in(splits[3], 71), 0),
        "target": noise(splits[2], (M, R), 1.0, 6.0, ((0, 4),), jnp.float32),
    }


def logsumexp_rows(values):
    top = lax.optimization_barrier(jnp.max(values, axis=1, keepdims=True))
    return jnp.log(lax.optimization_barrier(jnp.sum(jnp.exp(values - top), axis=1))) + top[:, 0]

def logsumexp_cols(values):
    top = lax.optimization_barrier(jnp.max(values, axis=0, keepdims=True))
    return jnp.log(lax.optimization_barrier(jnp.sum(jnp.exp(values - top), axis=0))) + top[0, :]

def reference(coupling, source, target):
    highest = lax.Precision.HIGHEST
    slab = jnp.dot(coupling, target, precision=highest, preferred_element_type=jnp.float32)
    factor = jnp.dot(source.T, slab, precision=highest, preferred_element_type=jnp.float32)
    factor = factor / math.sqrt(N * M)
    mapped = jnp.dot(source, factor, precision=highest, preferred_element_type=jnp.float32)
    logits = jnp.dot(mapped, target.T, precision=highest, preferred_element_type=jnp.float32) / R
    colpot = jnp.zeros((M,), jnp.float32)
    rowpot = jnp.zeros((N,), jnp.float32)
    for sweep in range(SWEEPS):
        rowpot = math.log(M) - logsumexp_rows(logits + colpot[None, :])
        colpot = math.log(N) - logsumexp_cols(logits + rowpot[:, None])
    return logits + rowpot[:, None] + colpot[None, :]
```

```python
import functools
import math

import jax
import jax.numpy as jnp
from jax import lax
from jax.experimental import pallas as pl
from jax.experimental.pallas import tpu as pltpu
from jax.sharding import PartitionSpec as P

R = 256
SWEEPS = 3
LANES = 128
SUB = 8
DEPTH = 512
WIDE = 256
MESH = pl.DeviceIdType.MESH
HIGHEST = lax.Precision.HIGHEST


def tree(op, values):
    while len(values) > 1:
        paired = [op(a, b) for a, b in zip(values[::2], values[1::2])]
        values = paired + values[len(paired) * 2 :]
    return values[0]


def split(x):
    high = x.astype(jnp.bfloat16)
    return high, (x - high.astype(jnp.float32)).astype(jnp.bfloat16)


def dot3(left, right, dims):
    (lh, ll), (rh, rl) = left, right
    dot = functools.partial(
        lax.dot_general, dimension_numbers=(dims, ((), ())), preferred_element_type=jnp.float32
    )
    return dot(lh, rh) + (dot(lh, rl) + dot(ll, rh))


def lse_fold(top, total, axis):
    peak = jnp.max(top, axis=axis, keepdims=True)
    return peak + jnp.log(jnp.sum(total * jnp.exp(top - peak), axis=axis, keepdims=True))


def lse_merge(parts):
    peak = tree(jnp.maximum, parts)
    return peak + jnp.log(tree(jnp.add, [jnp.exp(part - peak) for part in parts]))


def step_kernel(
    nr, nc, owners,
    coupling_hbm, source_hbm, target_hbm,
    logits_hbm, rowpot_out, colpot_out,
    coupling, source, target, high, low, logits, slab, factor_part, factor,
    from_cols, part, from_rows, piece,
    row_top, row_sum, col_top, col_sum,
    row_send, row_recv, col_send, col_recv,
    load_sems, logits_sem,
    a_send, a_recv, b_send, b_recv, c_send, c_recv, d_send, d_recv,
    rs_send, rs_recv, cs_send, cs_recv,
):
    rows, cols = logits.shape
    total_rows, total_cols = rows * nr, cols * nc
    mr, mc = lax.axis_index("rows"), lax.axis_index("cols")
    depths = cols // DEPTH
    tiles, chunks, blocks = cols // LANES, rows // LANES, LANES // SUB

    def span(at, size):
        return pl.ds(pl.multiple_of(at * size, size), size)

    def load_target(k):
        return pltpu.make_async_copy(
            target_hbm.at[span(k, DEPTH), :], target.at[span(k, DEPTH), :], load_sems.at[0, k]
        )

    def load_coupling(k):
        return pltpu.make_async_copy(
            coupling_hbm.at[:, span(k, DEPTH)], coupling.at[:, span(k, DEPTH)], load_sems.at[1, k]
        )

    load_source = pltpu.make_async_copy(source_hbm, source, load_sems.at[0, depths])
    for k in range(depths):
        load_target(k).start()
        load_coupling(k).start()
    load_source.start()

    def on_rows(d):
        return lax.rem(mr + d, nr)

    def on_cols(d):
        return lax.rem(mc + d, nc)

    barrier = pltpu.get_barrier_semaphore()
    for d in range(1, nc):
        pl.semaphore_signal(barrier, inc=1, device_id=(mr, on_cols(d)), device_id_type=MESH)
    for d in range(1, nr):
        pl.semaphore_signal(barrier, inc=1, device_id=(on_rows(d), mc), device_id_type=MESH)

    def remote(src, dst, send_sem, recv_sem, device):
        return pltpu.make_async_remote_copy(
            src_ref=src, dst_ref=dst, send_sem=send_sem, recv_sem=recv_sem,
            device_id=device, device_id_type=MESH,
        )

    def owned(index, act):
        if owners == nr:
            act()
        else:
            pl.when(index < owners)(act)

    slab[...] = jnp.zeros_like(slab)

    @pl.loop(0, depths)
    def _(k):
        load_target(k).wait()
        here = span(k, DEPTH)
        th, tl = split(target[here, :])
        high[here, :] = th
        low[here, :] = tl
        load_coupling(k).wait()
        slab[...] += dot3(split(coupling[:, here]), (th, tl), ((1,), (0,)))

    load_source.wait()
    factor_part[...] = lax.dot_general(
        source[...], slab[...], (((0,), (0,)), ((), ())),
        precision=HIGHEST, preferred_element_type=jnp.float32,
    )

    pl.semaphore_wait(barrier, nc - 1 + nr - 1)

    share = R // nc
    small = share // owners
    own_cols = span(mc, share)

    def copy_a(d):
        peer = on_cols(d)
        return remote(
            factor_part.at[span(peer, share), :], from_cols.at[d - 1],
            a_send.at[d - 1], a_recv.at[d - 1], (mr, peer),
        )

    for d in range(1, nc):
        copy_a(d).start()
    for d in range(1, nc):
        copy_a(d).wait_recv()
    part[...] = factor_part[own_cols, :] + tree(jnp.add, [from_cols[d] for d in range(nc - 1)])

    def copy_b(d):
        peer = on_rows(d)
        return peer, remote(
            part.at[span(peer, small), :], from_rows.at[d - 1],
            b_send.at[d - 1], b_recv.at[d - 1], (peer, mc),
        )

    for d in range(1, nr):
        peer, copy = copy_b(d)
        owned(peer, copy.start)

    def own_piece():
        for d in range(1, nr):
            copy_b(d)[1].wait_recv()
        total = part[span(mr, small), :] + tree(jnp.add, [from_rows[d] for d in range(nr - 1)])
        piece[...] = total
        factor[pl.ds(pl.multiple_of(mc * share + mr * small, small), small), :] = total

    owned(mr, own_piece)

    def copy_c(d):
        here = pl.ds(pl.multiple_of(mc * share + mr * small, small), small)
        return remote(
            piece, factor.at[here, :], c_send.at[d - 1], c_recv.at[d - 1], (on_rows(d), mc)
        )

    def spread():
        for d in range(1, nr):
            copy_c(d).start()

    owned(mr, spread)
    for d in range(1, nr):
        owned(lax.rem(mr + nr - d, nr), copy_c(d).wait_recv)

    def copy_d(d):
        return remote(
            factor.at[own_cols, :], factor.at[own_cols, :],
            d_send.at[d - 1], d_recv.at[d - 1], (mr, on_cols(d)),
        )

    for d in range(1, nc):
        copy_d(d).start()
    for d in range(1, nc):
        copy_d(d).wait_recv()

    scaled = factor[...] * (1.0 / math.sqrt(total_rows * total_cols))
    mapped = jnp.dot(
        source[...], scaled, precision=HIGHEST, preferred_element_type=jnp.float32
    ) * (1.0 / R)
    mapped = split(mapped)

    @pl.loop(0, cols // WIDE)
    def _(j):
        here = span(j, WIDE)
        logits[:, here] = dot3(mapped, (high[here, :], low[here, :]), ((1,), (1,)))

    store_logits = pltpu.make_async_copy(logits, logits_hbm, logits_sem)
    store_logits.start()

    colpot_out[...] = jnp.zeros_like(colpot_out)

    def row_copy(sweep, d):
        return remote(
            row_send.at[sweep], row_recv.at[sweep, d - 1],
            rs_send.at[sweep, d - 1], rs_recv.at[sweep, d - 1], (mr, on_cols(d)),
        )

    def col_copy(sweep, d):
        return remote(
            col_send.at[sweep], col_recv.at[sweep, d - 1],
            cs_send.at[sweep, d - 1], cs_recv.at[sweep, d - 1], (on_rows(d), mc),
        )

    def lane(t):
        return slice(t * LANES, (t + 1) * LANES)

    @pl.loop(0, SWEEPS)
    def _(sweep):
        @pl.loop(0, rows // SUB, unroll=4)
        def _(b):
            here = span(b, SUB)
            values = [logits[here, lane(t)] + colpot_out[:, lane(t)] for t in range(tiles)]
            top = tree(jnp.maximum, values)
            row_top[here, :] = top
            row_sum[here, :] = tree(jnp.add, [jnp.exp(value - top) for value in values])

        for c in range(chunks):
            row_send[sweep, c : c + 1, :] = lse_fold(
                row_top[lane(c), :].T, row_sum[lane(c), :].T, 0
            )
        for d in range(1, nc):
            row_copy(sweep, d).start()
        for d in range(1, nc):
            row_copy(sweep, d).wait_recv()
        lse = lse_merge([row_send[sweep]] + [row_recv[sweep, d] for d in range(nc - 1)])
        rowpot = math.log(total_cols) - lse
        for c in range(chunks):
            rowpot_out[lane(c), :] = jnp.broadcast_to(rowpot[c : c + 1, :], (LANES, LANES)).T

        @pl.loop(0, tiles)
        def _(t):
            here = span(t, LANES)
            top = total = None
            for c in range(chunks):
                values = []
                for b in range(blocks):
                    block = slice(c * LANES + b * SUB, c * LANES + (b + 1) * SUB)
                    values.append(logits[block, here] + rowpot_out[block, :])
                peak = tree(jnp.maximum, values if top is None else values + [top])
                fresh = tree(jnp.add, [jnp.exp(value - peak) for value in values])
                total = fresh if top is None else total * jnp.exp(top - peak) + fresh
                top = peak
            col_top[t] = top
            col_sum[t] = total

        for t in range(tiles):
            col_send[sweep, t : t + 1, :] = lse_fold(col_top[t], col_sum[t], 0)
        for d in range(1, nr):
            col_copy(sweep, d).start()
        for d in range(1, nr):
            col_copy(sweep, d).wait_recv()
        lse = lse_merge([col_send[sweep]] + [col_recv[sweep, d] for d in range(nr - 1)])
        colpot = math.log(total_rows) - lse
        for t in range(tiles):
            colpot_out[:, lane(t)] = jnp.broadcast_to(colpot[t : t + 1, :], (SUB, LANES))

    for d in range(1, nc):
        copy_a(d).wait_send()
        copy_d(d).wait_send()
        for sweep in range(SWEEPS):
            row_copy(sweep, d).wait_send()
    for d in range(1, nr):
        peer, copy = copy_b(d)
        owned(peer, copy.wait_send)
        owned(mr, copy_c(d).wait_send)
        for sweep in range(SWEEPS):
            col_copy(sweep, d).wait_send()
    store_logits.wait()


def finish_kernel(logits, rowpot, colpot, out):
    for t in range(logits.shape[1] // LANES):
        here = slice(t * LANES, (t + 1) * LANES)
        out[:, here] = logits[:, here] + rowpot[...] + colpot[0:1, here]


def on_device(nr, nc, coupling, source, target):
    rows, cols = coupling.shape
    share = R // nc
    owners = min(nr, share // SUB)
    small = share // owners
    tiles, chunks = cols // LANES, rows // LANES
    f32 = jnp.float32
    dma = pltpu.SemaphoreType.DMA
    vmem, anywhere = pl.BlockSpec(memory_space=pltpu.VMEM), pl.BlockSpec(memory_space=pl.ANY)
    logits, rowpot, colpot = pl.pallas_call(
        functools.partial(step_kernel, nr, nc, owners),
        out_shape=(
            jax.ShapeDtypeStruct((rows, cols), f32),
            jax.ShapeDtypeStruct((rows, LANES), f32),
            jax.ShapeDtypeStruct((SUB, cols), f32),
        ),
        in_specs=[anywhere] * 3,
        out_specs=(anywhere, vmem, vmem),
        scratch_shapes=[
            pltpu.VMEM((rows, cols), f32),
            pltpu.VMEM((rows, R), f32),
            pltpu.VMEM((cols, R), f32),
            pltpu.VMEM((cols, R), jnp.bfloat16),
            pltpu.VMEM((cols, R), jnp.bfloat16),
            pltpu.VMEM((rows, cols), f32),
            pltpu.VMEM((rows, R), f32),
            pltpu.VMEM((R, R), f32),
            pltpu.VMEM((R, R), f32),
            pltpu.VMEM((nc - 1, share, R), f32),
            pltpu.VMEM((share, R), f32),
            pltpu.VMEM((nr - 1, small, R), f32),
            pltpu.VMEM((small, R), f32),
            pltpu.VMEM((rows, LANES), f32),
            pltpu.VMEM((rows, LANES), f32),
            pltpu.VMEM((tiles, SUB, LANES), f32),
            pltpu.VMEM((tiles, SUB, LANES), f32),
            pltpu.VMEM((SWEEPS, chunks, LANES), f32),
            pltpu.VMEM((SWEEPS, nc - 1, chunks, LANES), f32),
            pltpu.VMEM((SWEEPS, tiles, LANES), f32),
            pltpu.VMEM((SWEEPS, nr - 1, tiles, LANES), f32),
            dma((2, cols // DEPTH + 1)),
            dma,
            dma((nc - 1,)), dma((nc - 1,)),
            dma((nr - 1,)), dma((nr - 1,)),
            dma((nr - 1,)), dma((nr - 1,)),
            dma((nc - 1,)), dma((nc - 1,)),
            dma((SWEEPS, nc - 1)), dma((SWEEPS, nc - 1)),
            dma((SWEEPS, nr - 1)), dma((SWEEPS, nr - 1)),
        ],
        compiler_params=pltpu.CompilerParams(
            collective_id=0, has_side_effects=True, vmem_limit_bytes=40 * 1024 * 1024
        ),
        name="sinkhorn_step",
    )(coupling, source, target)
    height = rows // 8
    return pl.pallas_call(
        finish_kernel,
        out_shape=jax.ShapeDtypeStruct((rows, cols), f32),
        grid=(rows // height,),
        in_specs=[
            pl.BlockSpec((height, cols), lambda i: (i, 0)),
            pl.BlockSpec((height, LANES), lambda i: (i, 0)),
            pl.BlockSpec((SUB, cols), lambda i: (0, 0)),
        ],
        out_specs=pl.BlockSpec((height, cols), lambda i: (i, 0)),
        name="add_potentials",
    )(logits, rowpot, colpot)


def solution(mesh):
    placed = (P("rows", "cols"), P("rows", None), P("cols", None))
    body = functools.partial(on_device, mesh.shape["rows"], mesh.shape["cols"])
    return jax.shard_map(
        body, mesh=mesh, in_specs=placed, out_specs=P("rows", "cols"), check_vma=False
    )
```

```python
import functools
import math

import jax
import jax.numpy as jnp
from jax import lax
from jax.experimental import pallas as pl
from jax.experimental.pallas import tpu as pltpu
from jax.sharding import PartitionSpec as P

R = 256
SWEEPS = 3
LANES = 128
SUB = 8
DEPTH = 1024
WIDE = 512
PARTS = 2
STORES = 4
MESH = pl.DeviceIdType.MESH


def tree(op, values):
    while len(values) > 1:
        paired = [op(a, b) for a, b in zip(values[::2], values[1::2])]
        values = paired + values[len(paired) * 2 :]
    return values[0]


def split(x):
    high = x.astype(jnp.bfloat16)
    return high, (x - high.astype(jnp.float32)).astype(jnp.bfloat16)


def dot3(left, right, dims):
    (lh, ll), (rh, rl) = left, right
    dot = functools.partial(
        lax.dot_general, dimension_numbers=(dims, ((), ())), preferred_element_type=jnp.float32
    )
    return dot(lh, rh) + (dot(lh, rl) + dot(ll, rh))


def lse_fold(top, total, axis):
    peak = jnp.max(top, axis=axis, keepdims=True)
    return peak + jnp.log(jnp.sum(total * jnp.exp(top - peak), axis=axis, keepdims=True))


def lse_merge(parts):
    peak = tree(jnp.maximum, parts)
    return peak + jnp.log(tree(jnp.add, [jnp.exp(part - peak) for part in parts]))


def step_kernel(
    nr, nc, owners,
    coupling, source, target,
    logits, rowpot_out, colpot_out,
    high, low, slab, factor_part, factor,
    from_cols, part, from_rows, piece,
    row_top, row_sum, col_top, col_sum,
    row_send, row_recv, col_send, col_recv,
    a_send, a_recv, b_send, b_recv, c_send, c_recv, d_send, d_recv,
    rs_send, rs_recv, cs_send, cs_recv,
):
    rows, cols = logits.shape
    total_rows, total_cols = rows * nr, cols * nc
    mr, mc = lax.axis_index("rows"), lax.axis_index("cols")
    tiles, blocks = cols // LANES, LANES // SUB
    chunks, half = rows // LANES // PARTS, tiles // PARTS

    def span(at, size):
        return pl.ds(pl.multiple_of(at * size, size), size)

    def lane(t):
        return slice(t * LANES, (t + 1) * LANES)

    def on_rows(d):
        return lax.rem(mr + d, nr)

    def on_cols(d):
        return lax.rem(mc + d, nc)

    row_peers = sorted(range(1, nr), key=lambda d: abs(2 * d - nr))
    col_peers = sorted(range(1, nc), key=lambda d: abs(2 * d - nc))

    barrier = pltpu.get_barrier_semaphore()
    for d in col_peers:
        pl.semaphore_signal(barrier, inc=1, device_id=(mr, on_cols(d)), device_id_type=MESH)
    for d in row_peers:
        pl.semaphore_signal(barrier, inc=1, device_id=(on_rows(d), mc), device_id_type=MESH)

    def remote(src, dst, send_sem, recv_sem, device):
        return pltpu.make_async_remote_copy(
            src_ref=src, dst_ref=dst, send_sem=send_sem, recv_sem=recv_sem,
            device_id=device, device_id_type=MESH,
        )

    def owned(index, act):
        if owners == nr:
            act()
        else:
            pl.when(index < owners)(act)

    slab[...] = jnp.zeros_like(slab)

    @pl.loop(0, cols // DEPTH)
    def _(k):
        here = span(k, DEPTH)
        slab[...] += dot3(split(coupling[:, here]), split(target[here, :]), ((1,), (0,)))

    whole = dot3(split(source[...].T), split(slab[...]), ((1,), (0,)))
    for h in range(PARTS):
        factor_part[h] = whole[:, lane(h)]

    pl.semaphore_wait(barrier, nc - 1 + nr - 1)

    share = R // nc
    small = share // owners
    own_cols = span(mc, share)
    own_rows = pl.ds(pl.multiple_of(mc * share + mr * small, small), small)

    def copy_a(h, d):
        peer = on_cols(d)
        return remote(
            factor_part.at[h, span(peer, share), :], from_cols.at[h, d - 1],
            a_send.at[h, d - 1], a_recv.at[h, d - 1], (mr, peer),
        )

    def copy_b(h, d):
        peer = on_rows(d)
        return peer, remote(
            part.at[h, span(peer, small), :], from_rows.at[h, d - 1],
            b_send.at[h, d - 1], b_recv.at[h, d - 1], (peer, mc),
        )

    def copy_c(h, d):
        return remote(
            piece.at[h], factor.at[h, own_rows, :],
            c_send.at[h, d - 1], c_recv.at[h, d - 1], (on_rows(d), mc),
        )

    def copy_d(h, d):
        return remote(
            factor.at[h, own_cols, :], factor.at[h, own_cols, :],
            d_send.at[h, d - 1], d_recv.at[h, d - 1], (mr, on_cols(d)),
        )

    for h in range(PARTS):
        for d in col_peers:
            copy_a(h, d).start()

    @pl.loop(0, cols // WIDE)
    def _(j):
        here = span(j, WIDE)
        high[:, here], low[:, here] = split(target[here, :].T)

    for h in range(PARTS):
        for d in col_peers:
            copy_a(h, d).wait_recv()
        part[h] = factor_part[h, own_cols, :] + tree(
            jnp.add, [from_cols[h, d] for d in range(nc - 1)]
        )
        for d in row_peers:
            peer, copy = copy_b(h, d)
            owned(peer, copy.start)

    for h in range(PARTS):
        def own_piece():
            for d in row_peers:
                copy_b(h, d)[1].wait_recv()
            total = part[h, span(mr, small), :] + tree(
                jnp.add, [from_rows[h, d] for d in range(nr - 1)]
            )
            piece[h] = total
            factor[h, own_rows, :] = total
            for d in row_peers:
                copy_c(h, d).start()

        owned(mr, own_piece)

    for h in range(PARTS):
        for d in row_peers:
            owned(lax.rem(mr + nr - d, nr), copy_c(h, d).wait_recv)
        for d in col_peers:
            copy_d(h, d).start()

    for h in range(PARTS):
        for d in col_peers:
            copy_d(h, d).wait_recv()

    scaled = jnp.concatenate([factor[h] for h in range(PARTS)], axis=1) * (
        1.0 / math.sqrt(total_rows * total_cols)
    )
    mapped = split(dot3(split(source[...]), split(scaled), ((1,), (0,))) * (1.0 / R))

    @pl.loop(0, cols // WIDE)
    def _(j):
        here = span(j, WIDE)
        logits[:, here] = dot3(mapped, (high[:, here], low[:, here]), ((1,), (0,)))

    def row_copy(sweep, g, d):
        return remote(
            row_send.at[sweep, g], row_recv.at[sweep, g, d - 1],
            rs_send.at[sweep, g, d - 1], rs_recv.at[sweep, g, d - 1], (mr, on_cols(d)),
        )

    def col_copy(sweep, h, d):
        return remote(
            col_send.at[sweep, h], col_recv.at[sweep, h, d - 1],
            cs_send.at[sweep, h, d - 1], cs_recv.at[sweep, h, d - 1], (on_rows(d), mc),
        )

    def absorb(values, held):
        top = tree(jnp.maximum, values if held is None else values + [held[0]])
        total = tree(jnp.add, [jnp.exp(value - top) for value in values])
        if held is not None:
            total = total + held[1] * jnp.exp(held[0] - top)
        return top, total

    def row_scan(first, count, seen, fresh, shifted):
        @pl.loop(0, count // SUB, unroll=4)
        def _(b):
            here = pl.ds(pl.multiple_of(first + b * SUB, SUB), SUB)
            values = [logits[here, lane(t)] for t in seen]
            if shifted:
                values = [value + colpot_out[:, lane(t)] for value, t in zip(values, seen)]
            held = None if fresh else (row_top[here, :], row_sum[here, :])
            row_top[here, :], row_sum[here, :] = absorb(values, held)

    def row_share(sweep, g):
        for c in range(chunks):
            here = lane(g * chunks + c)
            row_send[sweep, g, c : c + 1, :] = lse_fold(row_top[here, :].T, row_sum[here, :].T, 0)
        for d in col_peers:
            row_copy(sweep, g, d).start()

    def row_finish(sweep, g):
        for d in col_peers:
            row_copy(sweep, g, d).wait_recv()
        lse = lse_merge([row_send[sweep, g]] + [row_recv[sweep, g, d] for d in range(nc - 1)])
        rowpot = math.log(total_cols) - lse
        for c in range(chunks):
            rowpot_out[lane(g * chunks + c), :] = jnp.broadcast_to(
                rowpot[c : c + 1, :], (LANES, LANES)
            ).T

    def col_scan(g, first, count, fresh):
        @pl.loop(first, first + count)
        def _(t):
            here = span(t, LANES)
            held = None if fresh else (col_top[t], col_sum[t])
            for c in range(g * chunks, (g + 1) * chunks):
                spots = [
                    slice(c * LANES + b * SUB, c * LANES + (b + 1) * SUB) for b in range(blocks)
                ]
                held = absorb([logits[at, here] + rowpot_out[at, :] for at in spots], held)
            col_top[t], col_sum[t] = held

    def col_share(sweep, h):
        for t in range(half):
            at = h * half + t
            col_send[sweep, h, t : t + 1, :] = lse_fold(col_top[at], col_sum[at], 0)
        for d in row_peers:
            col_copy(sweep, h, d).start()

    def col_finish(sweep, h):
        for d in row_peers:
            col_copy(sweep, h, d).wait_recv()
        lse = lse_merge([col_send[sweep, h]] + [col_recv[sweep, h, d] for d in range(nr - 1)])
        colpot = math.log(total_rows) - lse
        for t in range(half):
            colpot_out[:, lane(h * half + t)] = jnp.broadcast_to(colpot[t : t + 1, :], (SUB, LANES))

    height = rows // PARTS
    for sweep in range(SWEEPS):
        if sweep == 0:
            for g in range(PARTS):
                row_scan(g * height, height, range(tiles), True, False)
                row_share(sweep, g)
        else:
            for h in range(PARTS):
                col_finish(sweep - 1, h)
                seen = range(h * half, (h + 1) * half)
                if h < PARTS - 1:
                    row_scan(0, rows, seen, h == 0, True)
            for g in range(PARTS):
                row_scan(g * height, height, seen, False, True)
                row_share(sweep, g)
        for g in range(PARTS - 1):
            row_finish(sweep, g)
            col_scan(g, 0, tiles, g == 0)
        row_finish(sweep, PARTS - 1)
        for h in range(PARTS):
            col_scan(PARTS - 1, h * half, half, False)
            col_share(sweep, h)
    for h in range(PARTS):
        col_finish(SWEEPS - 1, h)

    for h in range(PARTS):
        for d in col_peers:
            copy_a(h, d).wait_send()
            copy_d(h, d).wait_send()
            for sweep in range(SWEEPS):
                row_copy(sweep, h, d).wait_send()
        for d in row_peers:
            peer, copy = copy_b(h, d)
            owned(peer, copy.wait_send)
            owned(mr, copy_c(h, d).wait_send)
            for sweep in range(SWEEPS):
                col_copy(sweep, h, d).wait_send()


def finish_kernel(logits, rowpot, colpot, out, held, sems):
    height = logits.shape[0] // STORES

    def store(i):
        here = slice(i * height, (i + 1) * height)
        return pltpu.make_async_copy(held.at[here, :], out.at[here, :], sems.at[i])

    for i in range(STORES):
        here = slice(i * height, (i + 1) * height)
        for t in range(logits.shape[1] // LANES):
            lane = slice(t * LANES, (t + 1) * LANES)
            held[here, lane] = logits[here, lane] + rowpot[here, :] + colpot[0:1, lane]
        store(i).start()
    for i in range(STORES):
        store(i).wait()


def on_device(nr, nc, coupling, source, target):
    rows, cols = coupling.shape
    share = R // nc
    owners = min(nr, share // SUB)
    small = share // owners
    half, chunks = cols // LANES // PARTS, rows // LANES // PARTS
    tiles = cols // LANES
    f32 = jnp.float32
    dma = pltpu.SemaphoreType.DMA
    vmem, anywhere = pl.BlockSpec(memory_space=pltpu.VMEM), pl.BlockSpec(memory_space=pl.ANY)
    logits, rowpot, colpot = pl.pallas_call(
        functools.partial(step_kernel, nr, nc, owners),
        out_shape=(
            jax.ShapeDtypeStruct((rows, cols), f32),
            jax.ShapeDtypeStruct((rows, LANES), f32),
            jax.ShapeDtypeStruct((SUB, cols), f32),
        ),
        in_specs=[vmem] * 3,
        out_specs=(vmem, vmem, vmem),
        scratch_shapes=[
            pltpu.VMEM((R, cols), jnp.bfloat16),
            pltpu.VMEM((R, cols), jnp.bfloat16),
            pltpu.VMEM((rows, R), f32),
            pltpu.VMEM((PARTS, R, LANES), f32),
            pltpu.VMEM((PARTS, R, LANES), f32),
            pltpu.VMEM((PARTS, nc - 1, share, LANES), f32),
            pltpu.VMEM((PARTS, share, LANES), f32),
            pltpu.VMEM((PARTS, nr - 1, small, LANES), f32),
            pltpu.VMEM((PARTS, small, LANES), f32),
            pltpu.VMEM((rows, LANES), f32),
            pltpu.VMEM((rows, LANES), f32),
            pltpu.VMEM((tiles, SUB, LANES), f32),
            pltpu.VMEM((tiles, SUB, LANES), f32),
            pltpu.VMEM((SWEEPS, PARTS, chunks, LANES), f32),
            pltpu.VMEM((SWEEPS, PARTS, nc - 1, chunks, LANES), f32),
            pltpu.VMEM((SWEEPS, PARTS, half, LANES), f32),
            pltpu.VMEM((SWEEPS, PARTS, nr - 1, half, LANES), f32),
            dma((PARTS, nc - 1)), dma((PARTS, nc - 1)),
            dma((PARTS, nr - 1)), dma((PARTS, nr - 1)),
            dma((PARTS, nr - 1)), dma((PARTS, nr - 1)),
            dma((PARTS, nc - 1)), dma((PARTS, nc - 1)),
            dma((SWEEPS, PARTS, nc - 1)), dma((SWEEPS, PARTS, nc - 1)),
            dma((SWEEPS, PARTS, nr - 1)), dma((SWEEPS, PARTS, nr - 1)),
        ],
        compiler_params=pltpu.CompilerParams(
            collective_id=0, has_side_effects=True, vmem_limit_bytes=36 * 1024 * 1024
        ),
        name="sinkhorn_step",
    )(coupling, source, target)
    return pl.pallas_call(
        finish_kernel,
        out_shape=jax.ShapeDtypeStruct((rows, cols), f32),
        in_specs=[vmem] * 3,
        out_specs=anywhere,
        scratch_shapes=[pltpu.VMEM((rows, cols), f32), dma((STORES,))],
        compiler_params=pltpu.CompilerParams(vmem_limit_bytes=12 * 1024 * 1024),
        name="add_potentials",
    )(logits, rowpot, colpot)


def solution(mesh):
    placed = (P("rows", "cols"), P("rows", None), P("cols", None))
    body = functools.partial(on_device, mesh.shape["rows"], mesh.shape["cols"])
    return jax.shard_map(
        body, mesh=mesh, in_specs=placed, out_specs=P("rows", "cols"), check_vma=False
    )
```

```python
import functools
import math

import jax
import jax.numpy as jnp
from jax import lax
from jax.experimental import pallas as pl
from jax.experimental.pallas import tpu as pltpu
from jax.sharding import PartitionSpec as P

R = 256
SWEEPS = 3
LANES = 128
SUB = 8
LN2 = math.log(2.0)
DEPTH = 512
WIDE = 512
SPLITS = 2
PARTS = 1
STORES = 8
MESH = pl.DeviceIdType.MESH


def tree(op, values):
    while len(values) > 1:
        paired = [op(a, b) for a, b in zip(values[::2], values[1::2])]
        values = paired + values[len(paired) * 2 :]
    return values[0]


def split(x):
    high = x.astype(jnp.bfloat16)
    return high, (x - high.astype(jnp.float32)).astype(jnp.bfloat16)


def beside(x):
    high, low = split(x)
    return jnp.concatenate([high, high, low], axis=1)


def stacked(x):
    high, low = split(x)
    return jnp.concatenate([high, low, high], axis=0)


def dot3(left, right):
    return jnp.dot(left, right, preferred_element_type=jnp.float32)


def lse_fold(top, total, axis):
    peak = jnp.max(top, axis=axis, keepdims=True)
    return peak + jnp.log(jnp.sum(total * jnp.exp2(top - peak), axis=axis, keepdims=True)) * (1.0 / LN2)


def lse_merge(parts):
    peak = tree(jnp.maximum, parts)
    return peak + jnp.log(tree(jnp.add, [jnp.exp2(part - peak) for part in parts])) * (1.0 / LN2)


def step_kernel(
    nr, nc, owners,
    coupling_hbm, source_hbm, target_hbm,
    logits_hbm, rowpot_out, colpot_out,
    coupling, source, target, logits, load_sems, logits_sem,
    spread, slab, factor_part, factor,
    from_cols, part, from_rows, piece,
    row_top, row_sum, col_top, col_sum,
    row_send, row_recv, col_send, col_recv,
    a_send, a_recv, b_send, b_recv, c_send, c_recv, d_send, d_recv,
    rs_send, rs_recv, cs_send, cs_recv,
):
    rows, cols = logits.shape
    total_rows, total_cols = rows * nr, cols * nc
    mr, mc = lax.axis_index("rows"), lax.axis_index("cols")
    tiles, blocks = cols // LANES, LANES // SUB
    chunks, half = rows // LANES // PARTS, tiles // PARTS

    def span(at, size):
        return pl.ds(pl.multiple_of(at * size, size), size)

    def lane(t):
        return slice(t * LANES, (t + 1) * LANES)

    def on_rows(d):
        return lax.rem(mr + d, nr)

    def on_cols(d):
        return lax.rem(mc + d, nc)

    row_peers = sorted(range(1, nr), key=lambda d: -abs(2 * d - nr))
    col_peers = sorted(range(1, nc), key=lambda d: -abs(2 * d - nc))

    def load_target(k):
        return pltpu.make_async_copy(
            target_hbm.at[span(k, DEPTH), :], target.at[span(k, DEPTH), :], load_sems.at[0, k]
        )

    def load_coupling(k):
        return pltpu.make_async_copy(
            coupling_hbm.at[:, span(k, DEPTH)], coupling.at[:, span(k, DEPTH)], load_sems.at[1, k]
        )

    load_source = pltpu.make_async_copy(source_hbm, source, load_sems.at[0, cols // DEPTH])
    for k in range(cols // DEPTH):
        load_target(k).start()
        load_coupling(k).start()
    load_source.start()

    barrier = pltpu.get_barrier_semaphore()
    for d in col_peers:
        pl.semaphore_signal(barrier, inc=1, device_id=(mr, on_cols(d)), device_id_type=MESH)
    for d in row_peers:
        pl.semaphore_signal(barrier, inc=1, device_id=(on_rows(d), mc), device_id_type=MESH)

    def remote(src, dst, send_sem, recv_sem, device):
        return pltpu.make_async_remote_copy(
            src_ref=src, dst_ref=dst, send_sem=send_sem, recv_sem=recv_sem,
            device_id=device, device_id_type=MESH,
        )

    def settle(sized, sem):
        pltpu.make_async_copy(sized, sized, sem).wait()

    def owned(index, act):
        if owners == nr:
            act()
        else:
            pl.when(index < owners)(act)

    slab[...] = jnp.zeros_like(slab)

    @pl.loop(0, cols // DEPTH)
    def _(k):
        here = span(k, DEPTH)
        load_target(k).wait()
        load_coupling(k).wait()
        slab[...] += dot3(beside(coupling[:, here]), stacked(target[here, :]))

    load_source.wait()
    whole = dot3(beside(source[...].T), stacked(slab[...]))
    for h in range(SPLITS):
        factor_part[h] = whole[:, lane(h)]

    pl.semaphore_wait(barrier, nc - 1 + nr - 1)

    share = R // nc
    small = share // owners
    own_cols = span(mc, share)
    own_rows = pl.ds(pl.multiple_of(mc * share + mr * small, small), small)

    def copy_a(h, d):
        peer = on_cols(d)
        return remote(
            factor_part.at[h, span(peer, share), :], from_cols.at[h, d - 1],
            a_send.at[h], a_recv.at[h], (mr, peer),
        )

    def copy_b(h, d):
        peer = on_rows(d)
        return peer, remote(
            part.at[h, span(peer, small), :], from_rows.at[h, d - 1],
            b_send.at[h], b_recv.at[h], (peer, mc),
        )

    def copy_c(h, d):
        return remote(
            piece.at[h], factor.at[h, own_rows, :],
            c_send.at[h], c_recv.at[h], (on_rows(d), mc),
        )

    def copy_d(h, d):
        return remote(
            factor.at[h, own_cols, :], factor.at[h, own_cols, :],
            d_send.at[h], d_recv.at[h], (mr, on_cols(d)),
        )

    for h in range(SPLITS):
        for d in col_peers:
            copy_a(h, d).start()

    @pl.loop(0, cols // WIDE)
    def _(j):
        here = span(j, WIDE)
        spread[:, here] = stacked(target[here, :].T)

    for h in range(SPLITS):
        settle(from_cols.at[h], a_recv.at[h])
        part[h] = factor_part[h, own_cols, :] + tree(
            jnp.add, [from_cols[h, d] for d in range(nc - 1)]
        )
        for d in row_peers:
            peer, copy = copy_b(h, d)
            owned(peer, copy.start)

    for h in range(SPLITS):
        def own_piece():
            settle(from_rows.at[h], b_recv.at[h])
            total = part[h, span(mr, small), :] + tree(
                jnp.add, [from_rows[h, d] for d in range(nr - 1)]
            )
            piece[h] = total
            factor[h, own_rows, :] = total
            for d in row_peers:
                copy_c(h, d).start()

        owned(mr, own_piece)

    for h in range(SPLITS):
        if owners == nr:
            settle(from_rows.at[h], c_recv.at[h])
        else:
            for d in row_peers:
                owned(lax.rem(mr + nr - d, nr), copy_c(h, d).wait_recv)
        for d in col_peers:
            copy_d(h, d).start()

    for h in range(SPLITS):
        settle(from_cols.at[h], d_recv.at[h])

    scaled = jnp.concatenate([factor[h] for h in range(SPLITS)], axis=1) * (
        1.0 / math.sqrt(total_rows * total_cols)
    )
    mapped = beside(dot3(beside(source[...]), stacked(scaled)) * (1.0 / (R * LN2)))

    @pl.loop(0, cols // WIDE)
    def _(j):
        here = span(j, WIDE)
        logits[:, here] = dot3(mapped, spread[:, here])

    store_logits = pltpu.make_async_copy(logits, logits_hbm, logits_sem)
    store_logits.start()

    def row_copy(sweep, g, d):
        return remote(
            row_send.at[sweep, g], row_recv.at[sweep, g, d - 1],
            rs_send.at[sweep, g], rs_recv.at[sweep, g], (mr, on_cols(d)),
        )

    def col_copy(sweep, h, d):
        return remote(
            col_send.at[sweep, h], col_recv.at[sweep, h, d - 1],
            cs_send.at[sweep, h], cs_recv.at[sweep, h], (on_rows(d), mc),
        )

    def absorb(values, held):
        top = tree(jnp.maximum, values if held is None else values + [held[0]])
        total = tree(jnp.add, [jnp.exp2(value - top) for value in values])
        if held is not None:
            total = total + held[1] * jnp.exp2(held[0] - top)
        return top, total

    def row_scan(sweep, count, seen, shifted):
        for c in range(count // LANES):
            tops, sums = [], []
            for b in range(blocks):
                here = slice(c * LANES + b * SUB, c * LANES + (b + 1) * SUB)
                values = [logits[here, lane(t)] for t in seen]
                if shifted:
                    values = [value + colpot_out[:, lane(t)] for value, t in zip(values, seen)]
                top, total = absorb(values, None)
                tops.append(top)
                sums.append(total)
            tops, sums = jnp.concatenate(tops, axis=0).T, jnp.concatenate(sums, axis=0).T
            row_send[sweep, 0, c : c + 1, :] = lse_fold(tops, sums, 0)

    def row_share(sweep, g):
        for d in col_peers:
            row_copy(sweep, g, d).start()

    def row_finish(sweep, g):
        settle(row_recv.at[sweep, g], rs_recv.at[sweep, g])
        lse = lse_merge([row_send[sweep, g]] + [row_recv[sweep, g, d] for d in range(nc - 1)])
        rowpot = math.log2(total_cols) - lse
        for c in range(chunks):
            rowpot_out[lane(g * chunks + c), :] = jnp.broadcast_to(
                rowpot[c : c + 1, :], (LANES, LANES)
            ).T

    def col_scan(g, first, count, fresh):
        @pl.loop(first, first + count, unroll=4)
        def _(t):
            here = span(t, LANES)
            held = None if fresh else (col_top[t], col_sum[t])
            for c in range(g * chunks, (g + 1) * chunks):
                spots = [
                    slice(c * LANES + b * SUB, c * LANES + (b + 1) * SUB) for b in range(blocks)
                ]
                held = absorb([logits[at, here] + rowpot_out[at, :] for at in spots], held)
            col_top[t], col_sum[t] = held

    def col_share(sweep, h):
        for t in range(half):
            at = h * half + t
            col_send[sweep, h, t : t + 1, :] = lse_fold(col_top[at], col_sum[at], 0)
        for d in row_peers:
            col_copy(sweep, h, d).start()

    def col_finish(sweep, h):
        settle(col_recv.at[sweep, h], cs_recv.at[sweep, h])
        lse = lse_merge([col_send[sweep, h]] + [col_recv[sweep, h, d] for d in range(nr - 1)])
        colpot = math.log2(total_rows) - lse
        for t in range(half):
            colpot_out[:, lane(h * half + t)] = jnp.broadcast_to(colpot[t : t + 1, :], (SUB, LANES))

    height = rows // PARTS
    for sweep in range(SWEEPS):
        if sweep == 0:
            for g in range(PARTS):
                row_scan(sweep, height, range(tiles), False)
                row_share(sweep, g)
        else:
            for h in range(PARTS):
                col_finish(sweep - 1, h)
                seen = range(h * half, (h + 1) * half)
            for g in range(PARTS):
                row_scan(sweep, height, seen, True)
                row_share(sweep, g)
        for g in range(PARTS - 1):
            row_finish(sweep, g)
            col_scan(g, 0, tiles, g == 0)
        row_finish(sweep, PARTS - 1)
        for h in range(PARTS):
            col_scan(PARTS - 1, h * half, half, PARTS == 1)
            col_share(sweep, h)
    for h in range(PARTS):
        col_finish(SWEEPS - 1, h)

    for h in range(SPLITS):
        settle(from_cols.at[h], a_send.at[h])
        settle(from_cols.at[h], d_send.at[h])
        if owners == nr:
            settle(from_rows.at[h], b_send.at[h])
        else:
            for d in row_peers:
                peer, copy = copy_b(h, d)
                owned(peer, copy.wait_send)
        owned(mr, lambda: settle(from_rows.at[h], c_send.at[h]))
    for sweep in range(SWEEPS):
        for h in range(PARTS):
            settle(row_recv.at[sweep, h], rs_send.at[sweep, h])
            settle(col_recv.at[sweep, h], cs_send.at[sweep, h])
    store_logits.wait()


def finish_kernel(
    logits_hbm, rowpot_hbm, colpot_hbm, out_hbm, logits, rowpot, colpot, out, load_sems, store_sems
):
    height = logits.shape[0] // STORES

    def band(i):
        return slice(i * height, (i + 1) * height)

    def load(i):
        return pltpu.make_async_copy(
            logits_hbm.at[band(i), :], logits.at[band(i), :], load_sems.at[i]
        )

    def store(i):
        return pltpu.make_async_copy(out.at[band(i), :], out_hbm.at[band(i), :], store_sems.at[i])

    potentials = [
        pltpu.make_async_copy(rowpot_hbm, rowpot, load_sems.at[STORES]),
        pltpu.make_async_copy(colpot_hbm, colpot, load_sems.at[STORES + 1]),
    ]
    for copy in potentials:
        copy.start()
    for i in range(STORES):
        load(i).start()
    for copy in potentials:
        copy.wait()
    for i in range(STORES):
        load(i).wait()
        for t in range(logits.shape[1] // LANES):
            lane = slice(t * LANES, (t + 1) * LANES)
            total = logits[band(i), lane] + rowpot[band(i), :] + colpot[0:1, lane]
            out[band(i), lane] = total * LN2
        store(i).start()
    for i in range(STORES):
        store(i).wait()


def on_device(nr, nc, coupling, source, target):
    rows, cols = coupling.shape
    share = R // nc
    owners = min(nr, share // SUB)
    small = share // owners
    half, chunks = cols // LANES // PARTS, rows // LANES // PARTS
    tiles = cols // LANES
    f32 = jnp.float32
    dma = pltpu.SemaphoreType.DMA
    vmem, anywhere = pl.BlockSpec(memory_space=pltpu.VMEM), pl.BlockSpec(memory_space=pl.ANY)
    logits, rowpot, colpot = pl.pallas_call(
        functools.partial(step_kernel, nr, nc, owners),
        out_shape=(
            jax.ShapeDtypeStruct((rows, cols), f32),
            jax.ShapeDtypeStruct((rows, LANES), f32),
            jax.ShapeDtypeStruct((SUB, cols), f32),
        ),
        in_specs=[anywhere] * 3,
        out_specs=(anywhere, vmem, vmem),
        scratch_shapes=[
            pltpu.VMEM((rows, cols), f32),
            pltpu.VMEM((rows, R), f32),
            pltpu.VMEM((cols, R), f32),
            pltpu.VMEM((rows, cols), f32),
            dma((2, cols // DEPTH + 1)),
            dma,
            pltpu.VMEM((3 * R, cols), jnp.bfloat16),
            pltpu.VMEM((rows, R), f32),
            pltpu.VMEM((SPLITS, R, LANES), f32),
            pltpu.VMEM((SPLITS, R, LANES), f32),
            pltpu.VMEM((SPLITS, nc - 1, share, LANES), f32),
            pltpu.VMEM((SPLITS, share, LANES), f32),
            pltpu.VMEM((SPLITS, nr - 1, small, LANES), f32),
            pltpu.VMEM((SPLITS, small, LANES), f32),
            pltpu.VMEM((rows, LANES), f32),
            pltpu.VMEM((rows, LANES), f32),
            pltpu.VMEM((tiles, SUB, LANES), f32),
            pltpu.VMEM((tiles, SUB, LANES), f32),
            pltpu.VMEM((SWEEPS, PARTS, chunks, LANES), f32),
            pltpu.VMEM((SWEEPS, PARTS, nc - 1, chunks, LANES), f32),
            pltpu.VMEM((SWEEPS, PARTS, half, LANES), f32),
            pltpu.VMEM((SWEEPS, PARTS, nr - 1, half, LANES), f32),
            dma((SPLITS,)), dma((SPLITS,)),
            dma((SPLITS,)), dma((SPLITS,)),
            dma((SPLITS,)), dma((SPLITS,)),
            dma((SPLITS,)), dma((SPLITS,)),
            dma((SWEEPS, PARTS)), dma((SWEEPS, PARTS)),
            dma((SWEEPS, PARTS)), dma((SWEEPS, PARTS)),
        ],
        compiler_params=pltpu.CompilerParams(
            collective_id=0, has_side_effects=True, vmem_limit_bytes=60 * 1024 * 1024
        ),
        name="sinkhorn_step",
    )(coupling, source, target)
    return pl.pallas_call(
        finish_kernel,
        out_shape=jax.ShapeDtypeStruct((rows, cols), f32),
        in_specs=[anywhere] * 3,
        out_specs=anywhere,
        scratch_shapes=[
            pltpu.VMEM((rows, cols), f32),
            pltpu.VMEM((rows, LANES), f32),
            pltpu.VMEM((SUB, cols), f32),
            pltpu.VMEM((rows, cols), f32),
            dma((STORES + 2,)),
            dma((STORES,)),
        ],
        compiler_params=pltpu.CompilerParams(vmem_limit_bytes=60 * 1024 * 1024),
        name="add_potentials",
    )(logits, rowpot, colpot)


def solution(mesh):
    placed = (P("rows", "cols"), P("rows", None), P("cols", None))
    body = functools.partial(on_device, mesh.shape["rows"], mesh.shape["cols"])
    return jax.shard_map(
        body, mesh=mesh, in_specs=placed, out_specs=P("rows", "cols"), check_vma=False
    )
```
